256 devices in a mesh: blk: 64 (over z, y, core), lon: 4 (over x).
Axes of the slice: x: 4, y: 4, z: 8, core: 2. Of those that a mesh axis runs over, the one named last changes fastest.
Arguments:
- anomalies: float32 [16, 1152, 4320], P(None, 'blk', 'lon'), may hold values from -6 to 6
- classes: int32 [1152, 4320], P('blk', 'lon'), may hold values from 0 to 3
- legendre: float32 [256, 2160, 1152], P('blk', 'lon'), may hold values from -0.0078125 to 0.0078125
- precond: float32 [256, 16, 135, 135], P('blk', 'lon'), may hold values from -1 to 2, as said below
- prior: float32 [2160], P('lon'), may hold values from 0.05 to 0.5
- assign: int32 [256], replicated, may hold values from 0 to 255, as said below
Outputs:
- solution: float32 [256, 2, 16, 2160], P('blk', None, None, 'lon')
- residual: float32 [256, 2, 16, 2160], P('blk', None, None, 'lon')
The draws below stay inside these ranges and needn't reach their ends.
Inputs may be any that keep to these rules, and one draw needn't show every extreme that they name: `assign`: A permutation of the order indices; the 4 slots of each index of blk hold 2 pairs q and 255 - q. `precond`: each block is symmetric, and its diagonal entries exceed the sum of the magnitudes of the other entries of their row.
All inputs are finite; a program needn't handle non-finite values.
Results may differ from the reference program's by a relative error of at most 0.00026.
Values sent between devices are 32-bit elements; how exact they have to be, the bound alone decides.
No kernel may reach another device: no remote copies, remote signals or barrier semaphores. Data moves between devices by JAX's collectives and lax.ppermute only.
A program may use at most 128 MiB of HBM per device.

```python
import math
import jax
import jax.numpy as jnp
from jax import lax

L = 2160
NLON = 4320
NR = 1152
BLOCK = 135
ITERS = 2
NRHS = 16
M_WIN = 256
STRIDE = 8
NB = 16


def draw_precond(key, part):
    key_off = jax.random.fold_in(key, 11)
    key_diag = jax.random.fold_in(key, 12)
    raw_values = jax.random.uniform(key_off, (M_WIN, NB, BLOCK, BLOCK), jnp.float32, -1.0, 1.0) / BLOCK
    symmetric = 0.5 * (raw_values + jnp.swapaxes(raw_values, 2, 3))
    diagonal = jax.random.uniform(key_diag, (M_WIN, NB, BLOCK), jnp.float32, 1.0, 2.0)
    identity = jnp.eye(BLOCK, dtype=jnp.float32)
    return symmetric * (1.0 - identity) + diagonal[..., None] * identity


def draw_assign(key, part):
    half_count = M_WIN // 2
    shuffled = jax.random.permutation(jax.random.fold_in(key, 21), half_count)
    flip_bits = jax.random.randint(jax.random.fold_in(key, 22), (half_count,), 0, 2)
    first_slot = jnp.where(flip_bits == 1, M_WIN - 1 - shuffled, shuffled)
    second_slot = M_WIN - 1 - first_slot
    return jnp.stack([first_slot, second_slot], axis=1).reshape(M_WIN).astype(jnp.int32)


def set_ends(result, stream_key, low, top_value):
    shape = result.shape
    spot = [jax.random.randint(jax.random.fold_in(stream_key, axis), (), 0, shape[axis]) for axis in range(len(shape))]
    result = result.at[tuple(spot)].set(low)
    longest = shape.index(max(shape))
    spot[longest] = (spot[longest] + 1) % shape[longest]
    return result.at[tuple(spot)].set(top_value)


def block_scale(key, extent, shards, smallest, top_value):
    level, own = 1.0, jax.random.fold_in(key, 6)
    for axis_at, shards_of in shards:
        draws = jnp.exp(jax.random.uniform(jax.random.fold_in(own, axis_at), (shards_of,), jnp.float32, smallest / len(shards), top_value / len(shards)))
        level = level * jnp.repeat(draws, extent[axis_at] // shards_of).reshape([-1 if axis == axis_at else 1 for axis in range(len(extent))])
    return level


def centred(rng, dims, scale, limit, split=(), held_as=jnp.bfloat16):
    array = scale * jax.random.normal(rng, dims, jnp.float32)
    if split:
        array = array * block_scale(rng, dims, split, -0.22, 0.18)
    return jnp.clip(array, -limit, limit).astype(held_as)


def setup_inputs(seed: int = 0) -> dict:
    key_list = jax.random.split(jax.random.key(seed), 7)
    anomalies = centred(key_list[0], (NRHS, NR, NLON), 1.0, 6.0, ((1, 64), (2, 4)), jnp.float32)
    classes = set_ends(jax.random.randint(key_list[1], (NR, NLON), 0, 4), jax.random.fold_in(key_list[1], 1), 0, 3).astype(jnp.int32)
    legendre = centred(key_list[2], (M_WIN, L, NR), (L * M_WIN) ** -0.5, 0.0078125, ((0, 64), (1, 4)), jnp.float32)
    precond = draw_precond(jax.random.fold_in(key_list[6], 71), 0)
    prior = jnp.clip(jnp.exp(math.log(0.5) - 2.3025851 * jax.random.uniform(key_list[4], (L,), jnp.float32) ** block_scale(key_list[4], (L,), ((0, 4),), -0.2, 0.2)), 0.05, 0.5)
    assign = draw_assign(jax.random.fold_in(key_list[6], 71), 0)
    return {"anomalies": anomalies, "classes": classes, "legendre": legendre, "precond": precond, "prior": prior, "assign": assign}


HUBER_LEVELS = (1.0, 0.5, 0.25, 0.125)
HIGHEST = lax.Precision.HIGHEST


def build_mask(orders, first_degree, degrees):
    degree = first_degree + jnp.arange(degrees, dtype=jnp.int32)
    upper_part = (degree[None, :] >= orders[:, None]).astype(jnp.float32)
    sine_keep = upper_part * (orders[:, None] > 0).astype(jnp.float32)
    return jnp.stack([upper_part, sine_keep], axis=1)[:, :, None, :]


def trig_table(orders, first_col, columns, lon_total):
    column = first_col + jnp.arange(columns, dtype=jnp.int32)
    phases = (orders[:, None] * column[None, :]) % lon_total
    angles = phases.astype(jnp.float32) * (2.0 * math.pi / lon_total)
    return jnp.stack([jnp.cos(angles), jnp.sin(angles)], axis=1)


def huber_weights(classes):
    weighted = jnp.zeros(classes.shape, jnp.float32)
    for level_index in range(4):
        weighted = weighted + (classes == level_index).astype(jnp.float32) * HUBER_LEVELS[level_index]
    return weighted


def reference(anomalies, classes, legendre, precond, prior, assign):
    orders = (assign * STRIDE).astype(jnp.int32)
    live_mask = build_mask(orders, 0, L)
    trig_rows = trig_table(orders, 0, NLON, NLON)
    weights = huber_weights(classes)

    def forward(coeffs):
        cycles_part = jnp.einsum("scnl,slr->scnr", coeffs, legendre, precision=HIGHEST)
        return jnp.einsum("scnr,sck->nrk", cycles_part, trig_rows, precision=HIGHEST)

    def adjoint(grid_field):
        cycles_part = jnp.einsum("nrk,sck->scnr", grid_field, trig_rows, precision=HIGHEST)
        return jnp.einsum("scnr,slr->scnl", cycles_part, legendre, precision=HIGHEST)

    def normal(coeffs):
        return live_mask * (adjoint(weights[None] * forward(coeffs)) + prior * coeffs)

    def precondition(coeffs):
        blocks = coeffs.reshape(M_WIN, 2, NRHS, NB, BLOCK)
        applied = jnp.einsum("sbij,scnbj->scnbi", precond, blocks, precision=HIGHEST)
        return live_mask * applied.reshape(coeffs.shape)

    def column_dot(lhs_values, rhs_values):
        return jnp.sum(lhs_values * rhs_values, axis=(0, 1, 3))

    def spread(values):
        return values[None, None, :, None]

    residual = live_mask * adjoint(weights[None] * anomalies)
    solution = jnp.zeros_like(residual)
    search = precondition(residual)
    fit_now = column_dot(residual, search)
    direction = search
    for iteration in range(ITERS):
        image_vec = normal(direction)
        alpha_step = fit_now / column_dot(direction, image_vec)
        solution = solution + spread(alpha_step) * direction
        residual = residual - spread(alpha_step) * image_vec
        if iteration + 1 < ITERS:
            search = precondition(residual)
            fit_next = column_dot(residual, search)
            direction = search + spread(fit_next / fit_now) * direction
            fit_now = fit_next
    return solution, residual
```

```python
import functools
import math

import jax
import jax.numpy as jnp
from jax import lax
from jax.experimental import pallas as pl
from jax.experimental.pallas import tpu as pltpu
from jax.sharding import PartitionSpec as P

F32 = jnp.float32
BF16 = jnp.bfloat16
HUBER_LEVELS = (1.0, 0.5, 0.25, 0.125)

BLK = 64
LON = 4
SLOTS = 4
NRHS = 16
NLO = NRHS // LON
CYC = 18
CYC_PAD = 24
PERIOD = 540
PERIOD_PAD = 640
DEG = 540
NR = BLK * CYC
BLOCK = 135
GROUPS = DEG // BLOCK
SC = 2 * SLOTS
LANES = SC * NLO
MSG_ROWS = 5
XW = NR + 128
VMEM_LIMIT = 48 * 1024 * 1024
NN = (((1,), (0,)), ((), ()))
NT = (((1,), (1,)), ((), ()))
PERMS = [[(i, (i + s) % LON) for i in range(LON)] for s in range(1, LON)]


def split(x):
    hi = x.astype(BF16)
    return hi, (x - hi.astype(F32)).astype(BF16)


def dot(a, b, dims):
    return lax.dot_general(a, b, dims, preferred_element_type=F32)


def dot_split(a, b, dims):
    b_hi, b_lo = b
    a_hi, a_lo = split(a)
    rows = a.shape[0]
    both = dot(jnp.concatenate([a_hi, a_lo], axis=0), b_hi, dims)
    return both[:rows] + both[rows:] + dot(a_hi, b_lo, dims)


def call(kernel, out_shape, scratch=(), **kw):
    return pl.pallas_call(
        kernel,
        out_shape=out_shape,
        scratch_shapes=list(scratch),
        compiler_params=pltpu.CompilerParams(vmem_limit_bytes=VMEM_LIMIT),
        **kw,
    )


def shape(*dims):
    return jax.ShapeDtypeStruct(dims, F32)


def fold_kernel(lon_ref, anomalies_ref, classes_ref, *out_refs):
    lon = lon_ref[0]
    classes = classes_ref[...]
    weights = jnp.zeros(classes.shape, F32)
    for level, value in enumerate(HUBER_LEVELS):
        weights = weights + jnp.where(classes == level, value, 0.0)

    def fold(field):
        return field[:, :PERIOD] + field[:, PERIOD:]

    folded_weights = fold(weights)
    for shift, out in enumerate(out_refs):
        out[...] = jnp.zeros(out.shape, F32)
        group = lax.rem(lon + shift, LON)
        for column in range(NLO):
            row = column * CYC_PAD
            out[row : row + CYC, :PERIOD] = fold(anomalies_ref[group * NLO + column] * weights)
            if column < CYC // 6:
                out[row + CYC : row + CYC_PAD, :PERIOD] = folded_weights[column * 6 : column * 6 + 6]


def spread_rows(values, vt_ref, extras_hi, extras_lo):
    for sc in range(SC):
        for column in range(NLO):
            piece = values[column * CYC_PAD : column * CYC_PAD + CYC, sc * BLK : (sc + 1) * BLK]
            vt_ref[pl.ds(sc * NLO + column, CYC, stride=LANES), 0:BLK] = piece
    vt_ref[CYC * LANES : (CYC + 1) * LANES, 0:BLK] = extras_hi
    vt_ref[(CYC + 1) * LANES : (CYC + 2) * LANES, 0:BLK] = extras_lo


def write_messages(vt_ref, out_ref):
    for j in range(MSG_ROWS):
        turned = jnp.transpose(vt_ref[j * 128 : (j + 1) * 128, :])
        out_ref[pl.ds(j, BLK, stride=MSG_ROWS), :] = turned[:BLK]


def first_kernel(c0, c1, c2, c3, trig_ref, out_ref, weights_ref, vt_ref):
    total = c0[...] + c1[...] + c2[...] + c3[...]
    weights_ref[...] = jnp.zeros(weights_ref.shape, F32)
    for part in range(CYC // 6):
        weights_ref[part * 6 : part * 6 + 6, :] = total[
            part * CYC_PAD + CYC : (part + 1) * CYC_PAD
        ]
    spectrum = dot_split(total, split(trig_ref[...]), NT)
    zero = jnp.zeros((LANES, BLK), F32)
    vt_ref[...] = jnp.zeros(vt_ref.shape, F32)
    spread_rows(spectrum, vt_ref, zero, zero)
    write_messages(vt_ref, out_ref)


def grid_kernel(later, *refs):
    if later:
        msg_ref, trig_ref, weights_ref, old_ref, state_ref, out_ref, vt_ref, x_ref = refs
    else:
        msg_ref, trig_ref, weights_ref, out_ref, grid_ref, state_ref, vt_ref, x_ref = refs
    vt_ref[...] = jnp.zeros(vt_ref.shape, F32)
    x_ref[...] = jnp.zeros(x_ref.shape, F32)
    for j in range(MSG_ROWS):
        vt_ref[j * 128 : (j + 1) * 128, 0:BLK] = jnp.transpose(
            msg_ref[pl.ds(j, BLK, stride=MSG_ROWS), :]
        )
    for sc in range(SC):
        for column in range(NLO):
            x_ref[column * CYC_PAD : column * CYC_PAD + CYC, sc * BLK : (sc + 1) * BLK] = vt_ref[
                pl.ds(sc * NLO + column, CYC, stride=LANES), 0:BLK
            ]
    dots = jnp.sum(vt_ref[CYC * LANES : (CYC + 2) * LANES, 0:BLK], axis=1, keepdims=True)

    def total(start, step):
        value = dots[start : start + NLO]
        for at in range(start + step, start + LANES, step):
            value = value + dots[at : at + NLO]
        return value

    fit = total(0, NLO)
    prior_zz = total(LANES, 2 * NLO)
    if later:
        prior_zd = total(LANES + NLO, 2 * NLO)
    trig = split(trig_ref[...])
    field = dot_split(x_ref[...], trig, NN)
    if later:
        beta = fit / state_ref[0:NLO, 0:1]
        prior_term = prior_zz + 2.0 * beta * prior_zd + beta * beta * state_ref[NLO : 2 * NLO, 0:1]
        spread_beta = jnp.concatenate(
            [jnp.broadcast_to(beta[i : i + 1], (CYC_PAD, 1)) for i in range(NLO)], axis=0
        )
        field = field + spread_beta * old_ref[...]
    else:
        beta = jnp.zeros_like(fit)
        prior_term = prior_zz
        grid_ref[...] = field
        state_ref[...] = jnp.broadcast_to(jnp.concatenate([fit, prior_term], axis=0), state_ref.shape)
    weights = weights_ref[...]
    weighted = jnp.concatenate(
        [field[i * CYC_PAD : (i + 1) * CYC_PAD] * weights for i in range(NLO)], axis=0
    )
    square = jnp.sum(weighted * field, axis=1, keepdims=True)
    energy = jnp.concatenate(
        [
            jnp.sum(square[i * CYC_PAD : (i + 1) * CYC_PAD], axis=0, keepdims=True)
            for i in range(NLO)
        ],
        axis=0,
    )
    spectrum = dot_split(weighted, trig, NT)
    extras_hi = jnp.broadcast_to(jnp.concatenate([energy] * SC, axis=0), (LANES, BLK))
    extras_lo = jnp.broadcast_to(
        jnp.concatenate([fit, prior_term, beta] + [jnp.zeros_like(fit)] * (SC - 3), axis=0),
        (LANES, BLK),
    )
    spread_rows(spectrum, vt_ref, extras_hi, extras_lo)
    write_messages(vt_ref, out_ref)


def unpack_kernel(msg_ref, out_ref, yt_ref):
    yt_ref[NR:, :] = jnp.zeros((XW - NR, 128), F32)
    for j in range(MSG_ROWS):
        value = msg_ref[pl.ds(j, BLK, stride=MSG_ROWS), :]
        for q in range(128 // LANES):
            cycle = 4 * j + q
            turned = value if q == 0 else pltpu.roll(value, 128 - q * LANES, 1)
            if cycle < CYC:
                yt_ref[pl.ds(cycle, BLK, stride=CYC), :] = turned
            elif cycle == CYC:
                yt_ref[NR : NR + 1, :] = jnp.sum(turned, axis=0, keepdims=True)
            else:
                yt_ref[NR + 1 : NR + 2, :] = turned[0:1]
    for t in range(NR // 128):
        out_ref[:, t * 128 : (t + 1) * 128] = jnp.transpose(yt_ref[t * 128 : (t + 1) * 128, :])[
            :LANES
        ]
    tail = jnp.transpose(yt_ref[NR:, :])[:LANES]
    energy = tail[:, 0:1]
    fit, prior_term, beta = (
        jnp.concatenate([tail[i * NLO : (i + 1) * NLO, 1:2]] * SC, axis=0) for i in range(3)
    )
    alpha = fit / (energy + prior_term)
    lane = lax.broadcasted_iota(jnp.int32, (LANES, 128), 1)
    out_ref[:, NR:] = jnp.where(lane == 0, alpha, jnp.where(lane == 1, beta, 0.0))


def pack_kernel(y0, y1, y2, y3, out_ref, yt_ref):
    for t in range(XW // 128):
        cols = slice(t * 128, (t + 1) * 128)
        total = y0[:, cols] + y1[:, cols] + y2[:, cols] + y3[:, cols]
        yt_ref[cols, 0:LANES] = jnp.transpose(total)
    for j in range(MSG_ROWS):
        pieces = []
        for q in range(128 // LANES):
            cycle = 4 * j + q
            if cycle < CYC:
                pieces.append(yt_ref[pl.ds(cycle, BLK, stride=CYC), 0:LANES])
            else:
                at = NR + cycle - CYC
                pieces.append(jnp.broadcast_to(yt_ref[at : at + 1, 0:LANES], (BLK, LANES)))
        out_ref[pl.ds(j, BLK, stride=MSG_ROWS), :] = jnp.concatenate(pieces, axis=1)


def coefficient_kernel(stage, info_ref, *refs):
    refs = list(refs)
    chunks = [refs.pop(0) for _ in range(LON)]
    legendre_ref = refs.pop(0)
    prior_ref = refs.pop(0)
    slot = pl.program_id(0)
    lon = info_ref[0]
    order = info_ref[1 + slot]
    rows = LON * 2 * NLO

    degree = lon * DEG + lax.broadcasted_iota(jnp.int32, (rows, DEG), 1)
    row = lax.broadcasted_iota(jnp.int32, (rows, DEG), 0)
    sine = lax.rem(row // NLO, 2) == 1
    dead_sine = jnp.logical_and(sine, order == 0)
    live = jnp.logical_and(degree >= order, jnp.logical_not(dead_sine))

    cycles = jnp.concatenate([chunk[:, :NR] for chunk in chunks], axis=0)
    extras = jnp.concatenate([chunk[:, NR:] for chunk in chunks], axis=0)
    legendre = split(legendre_ref[0])
    image = dot_split(cycles, legendre, NT)
    prior = prior_ref[...]

    if stage == "last":
        res_ref, z_ref, d_ref, alpha_ref, sol_out, res_out = refs
        alpha, beta = extras[:, 0:1], extras[:, 1:2]
        old = d_ref[0]
        direction = z_ref[0] + beta * old
        image = jnp.where(live, image + prior * direction, 0.0)
        fitted = alpha_ref[0][:, 0:1] * old + alpha * direction
        residual = res_ref[0] - alpha * image
        for out, value in ((sol_out, fitted), (res_out, residual)):
            group = 2 * NLO
            parts = [value[i * group : (i + 1) * group] for i in range(LON)]
            for place in range(LON):
                shift = lax.rem(place - lon + LON, LON)
                chosen = parts[0]
                for i in range(1, LON):
                    chosen = jnp.where(shift == i, parts[i], chosen)
                for part in range(2):
                    out[0, part, place * NLO : (place + 1) * NLO, :] = chosen[
                        part * NLO : (part + 1) * NLO
                    ]
        return

    precond_ref = refs.pop(0)
    if stage == "first":
        res_out, z_out = refs[:2]
        y_refs = refs[2:]
        residual = jnp.where(live, image, 0.0)
    else:
        res_ref, d_ref, res_out, z_out, alpha_out = refs[:5]
        y_refs = refs[5:]
        alpha = extras[:, 0:1]
        old = d_ref[0]
        image = jnp.where(live, image + prior * old, 0.0)
        residual = res_ref[0] - alpha * image
        alpha_out[0] = jnp.broadcast_to(alpha, (rows, 128))
    applied = [
        dot_split(residual[:, g * BLOCK : (g + 1) * BLOCK], split(precond_ref[0, g]), NT)
        for g in range(GROUPS)
    ]
    search = jnp.where(live, jnp.concatenate(applied, axis=1), 0.0)
    res_out[0] = residual
    z_out[0] = search
    up = dot_split(search, legendre, NN)
    fit = jnp.sum(residual * search, axis=1, keepdims=True)
    prior_zz = jnp.sum(search * prior * search, axis=1, keepdims=True)
    if stage == "first":
        prior_zd = jnp.zeros_like(prior_zz)
    else:
        prior_zd = jnp.sum(search * prior * old, axis=1, keepdims=True)
    lane = lax.broadcasted_iota(jnp.int32, (2 * NLO, 128), 1)
    for shift, y_ref in enumerate(y_refs):
        at = shift * 2 * NLO
        y_ref[:, :NR] = up[at : at + 2 * NLO]
        both = jnp.concatenate(
            [
                prior_zz[at : at + NLO] + prior_zz[at + NLO : at + 2 * NLO],
                prior_zd[at : at + NLO] + prior_zd[at + NLO : at + 2 * NLO],
            ],
            axis=0,
        )
        y_ref[:, NR:] = jnp.where(
            lane == 0, fit[at : at + 2 * NLO], jnp.where(lane == 1, both, 0.0)
        )


def coefficient_step(stage, info, chunks, legendre, prior, arrays):
    rows = LON * 2 * NLO
    chunk_spec = pl.BlockSpec((2 * NLO, XW), lambda s, info: (s, 0))
    state_spec = pl.BlockSpec((1, rows, DEG), lambda s, info: (s, 0, 0))
    alpha_spec = pl.BlockSpec((1, rows, 128), lambda s, info: (s, 0, 0))
    precond_spec = pl.BlockSpec((1, GROUPS, BLOCK, BLOCK), lambda s, info: (s, 0, 0, 0))
    out_spec = pl.BlockSpec((1, 2, NRHS, DEG), lambda s, info: (s, 0, 0, 0))
    in_specs = [chunk_spec] * LON + [
        pl.BlockSpec((1, DEG, NR), lambda s, info: (s, 0, 0)),
        pl.BlockSpec((1, DEG), lambda s, info: (0, 0)),
    ]
    state = shape(SLOTS, rows, DEG)
    chunk = shape(2 * NLO * SLOTS, XW)
    if stage == "first":
        in_specs += [precond_spec]
        out_specs = [state_spec] * 2 + [chunk_spec] * LON
        out_shape = [state] * 2 + [chunk] * LON
    elif stage == "middle":
        in_specs += [precond_spec, state_spec, state_spec]
        out_specs = [state_spec] * 2 + [alpha_spec] + [chunk_spec] * LON
        out_shape = [state] * 2 + [shape(SLOTS, rows, 128)] + [chunk] * LON
    else:
        in_specs += [state_spec] * 3 + [alpha_spec]
        out_specs = [out_spec] * 2
        out_shape = [shape(SLOTS, 2, NRHS, DEG)] * 2
    return pl.pallas_call(
        functools.partial(coefficient_kernel, stage),
        out_shape=out_shape,
        grid_spec=pltpu.PrefetchScalarGridSpec(
            num_scalar_prefetch=1, grid=(SLOTS,), in_specs=in_specs, out_specs=out_specs
        ),
        compiler_params=pltpu.CompilerParams(
            vmem_limit_bytes=VMEM_LIMIT, dimension_semantics=("arbitrary",)
        ),
    )(info, *chunks, legendre, prior, *arrays)


def give_chunks(chunks):
    moved = [lax.ppermute(c, "lon", perm) for c, perm in zip(chunks[1:], PERMS)]
    return [chunks[0]] + moved


def gather_chunks(chunk):
    moved = [lax.ppermute(chunk, "lon", perm) for perm in PERMS]
    return [chunk] + moved[::-1]


def exchange(messages):
    sent = messages.reshape(BLK, 1, MSG_ROWS * 128)
    return lax.all_to_all(sent, "blk", 0, 0, tiled=True).reshape(BLK * MSG_ROWS, 128)


def trig_table(assign):
    index = assign.reshape(BLK, SLOTS).T.reshape(SLOTS, 1, BLK, 1) * 8
    column = jnp.arange(PERIOD_PAD, dtype=jnp.int32)
    angles = ((index * column) % (8 * PERIOD)).astype(F32) * (2.0 * math.pi / (8 * PERIOD))
    table = jnp.concatenate([jnp.cos(angles), jnp.sin(angles)], axis=1)
    return jnp.where(column < PERIOD, table, 0.0).reshape(SC * BLK, PERIOD_PAD)


def body(anomalies, classes, legendre, precond, prior, assign):
    lon = lax.axis_index("lon")
    own = lax.dynamic_slice_in_dim(assign, lax.axis_index("blk") * SLOTS, SLOTS) * 8
    info = jnp.concatenate([jnp.stack([lon]).astype(jnp.int32), own.astype(jnp.int32)])
    trig = trig_table(assign)
    prior_row = prior.reshape(1, DEG)
    messages = shape(BLK * MSG_ROWS, 128)
    vt = pltpu.VMEM((MSG_ROWS * 128, 128), F32)
    yt = pltpu.VMEM((XW, 128), F32)
    grid_rows = NLO * CYC_PAD
    x_scratch = pltpu.VMEM((grid_rows, SC * BLK), F32)
    smem = pl.BlockSpec(memory_space=pltpu.SMEM)
    vmem = pl.BlockSpec(memory_space=pltpu.VMEM)

    folded = call(
        fold_kernel,
        [shape(grid_rows, PERIOD_PAD)] * LON,
        in_specs=[smem, vmem, vmem],
    )(info, anomalies, classes)
    folded = give_chunks(folded)
    sent, weights = call(first_kernel, [messages, shape(CYC_PAD, PERIOD_PAD)], [vt])(*folded, trig)

    def to_coefficients(sent):
        unpacked = call(unpack_kernel, shape(LANES, XW), [yt])(exchange(sent))
        return gather_chunks(unpacked)

    def to_grid(chunks):
        return exchange(call(pack_kernel, messages, [yt])(*give_chunks(chunks)))

    res0, z0, *chunks = coefficient_step(
        "first", info, to_coefficients(sent), legendre, prior_row, [precond]
    )
    sent, field, state = call(
        functools.partial(grid_kernel, False),
        [messages, shape(grid_rows, PERIOD_PAD), shape(2 * NLO, 128)],
        [vt, x_scratch],
    )(to_grid(chunks), trig, weights)
    res1, z1, alpha0, *chunks = coefficient_step(
        "middle", info, to_coefficients(sent), legendre, prior_row, [precond, res0, z0]
    )
    sent = call(functools.partial(grid_kernel, True), messages, [vt, x_scratch])(
        to_grid(chunks), trig, weights, field, state
    )
    return tuple(
        coefficient_step(
            "last", info, to_coefficients(sent), legendre, prior_row, [res1, z1, z0, alpha0]
        )
    )


def solution(mesh):
    in_specs = (
        P(None, "blk", "lon"),
        P("blk", "lon"),
        P("blk", "lon", None),
        P("blk", "lon", None, None),
        P("lon"),
        P(),
    )
    out_specs = (P("blk", None, None, "lon"), P("blk", None, None, "lon"))
    return jax.shard_map(body, mesh=mesh, in_specs=in_specs, out_specs=out_specs, check_vma=False)
```

```python
import functools
import math

import jax
import jax.numpy as jnp
from jax import lax
from jax.experimental import pallas as pl
from jax.experimental.pallas import tpu as pltpu
from jax.sharding import PartitionSpec as P

F32 = jnp.float32
BF16 = jnp.bfloat16
HUBER_LEVELS = (1.0, 0.5, 0.25, 0.125)

BLK = 64
LON = 4
SLOTS = 4
NRHS = 16
NLO = NRHS // LON
CYC = 18
CYC_PAD = 24
PERIOD = 540
PERIOD_PAD = 640
DEG = 540
NR = BLK * CYC
BLOCK = 135
GROUPS = DEG // BLOCK
SC = 2 * SLOTS
LANES = SC * NLO
MSG_ROWS = 5
TILES = NR // 128
SIZE = 2 * NLO
ROWS = LON * SIZE
EXTRA = TILES * LANES
CHUNK_ROWS = EXTRA + SIZE
PREP_STEP = 128
VMEM_LIMIT = 24 * 1024 * 1024
NN = (((1,), (0,)), ((), ()))
NT = (((1,), (1,)), ((), ()))
PERMS = [[(i, (i + s) % LON) for i in range(LON)] for s in range(1, LON)]


def split(x):
    hi = x.astype(BF16)
    return hi, (x - hi.astype(F32)).astype(BF16)


def dot(a, b, dims):
    return lax.dot_general(a, b, dims, preferred_element_type=F32)


def dot_split(a, b, dims):
    b_hi, b_lo = b
    a_hi, a_lo = split(a)
    rows = a.shape[0]
    both = dot(jnp.concatenate([a_hi, a_lo], axis=0), b_hi, dims)
    return both[:rows] + both[rows:] + dot(a_hi, b_lo, dims)


def call(kernel, out_shape, scratch=(), **kw):
    return pl.pallas_call(
        kernel,
        out_shape=out_shape,
        scratch_shapes=list(scratch),
        compiler_params=pltpu.CompilerParams(vmem_limit_bytes=VMEM_LIMIT),
        **kw,
    )


def shape(*dims):
    return jax.ShapeDtypeStruct(dims, F32)


def fold_kernel(anomalies_ref, classes_ref, *refs):
    out_refs, by_column = refs[:-1], refs[-1]
    lon = lax.axis_index("lon")
    classes = classes_ref[...]
    weights = jnp.zeros(classes.shape, F32)
    for level, value in enumerate(HUBER_LEVELS):
        weights = weights + jnp.where(classes == level, value, 0.0)

    def fold(field):
        return field[:, :PERIOD] + field[:, PERIOD:]

    by_column[...] = jnp.zeros(by_column.shape, F32)
    for cycle in range(CYC):
        columns = fold(anomalies_ref[cycle] * weights[cycle : cycle + 1])
        for column in range(NRHS):
            by_column[column, cycle : cycle + 1, :PERIOD] = columns[column : column + 1]
    folded_weights = fold(weights)
    for shift, out in enumerate(out_refs):
        group = lax.rem(lon + shift, LON)
        for column in range(NLO):
            row = column * CYC_PAD
            out[row : row + CYC_PAD, :] = by_column[group * NLO + column]
            if column < CYC // 6:
                out[row + CYC : row + CYC_PAD, :PERIOD] = folded_weights[column * 6 : column * 6 + 6]


def spread_rows(values, vt_ref, extras_hi, extras_lo):
    for sc in range(SC):
        for column in range(NLO):
            piece = values[column * CYC_PAD : column * CYC_PAD + CYC, sc * BLK : (sc + 1) * BLK]
            vt_ref[pl.ds(sc * NLO + column, CYC, stride=LANES), 0:BLK] = piece
    vt_ref[CYC * LANES : (CYC + 1) * LANES, 0:BLK] = extras_hi
    vt_ref[(CYC + 1) * LANES : (CYC + 2) * LANES, 0:BLK] = extras_lo


def write_messages(vt_ref, out_ref):
    for j in range(MSG_ROWS):
        turned = jnp.transpose(vt_ref[j * 128 : (j + 1) * 128, :])
        out_ref[pl.ds(j, BLK, stride=MSG_ROWS), :] = turned[:BLK]


def first_kernel(c0, c1, c2, c3, hi_ref, lo_ref, done_ref, out_ref, weights_ref, vt_ref):
    total = c0[...] + c1[...] + c2[...] + c3[...]
    weights_ref[...] = jnp.zeros(weights_ref.shape, F32)
    for part in range(CYC // 6):
        weights_ref[part * 6 : part * 6 + 6, :] = total[
            part * CYC_PAD + CYC : (part + 1) * CYC_PAD
        ]
    spectrum = dot_split(total, (hi_ref[...], lo_ref[...]), NT)
    zero = jnp.zeros((LANES, BLK), F32)
    vt_ref[...] = jnp.zeros(vt_ref.shape, F32)
    spread_rows(spectrum, vt_ref, zero, zero)
    write_messages(vt_ref, out_ref)


def grid_kernel(later, *refs):
    if later:
        msg_ref, hi_ref, lo_ref, weights_ref, old_ref, state_ref, out_ref, vt_ref, x_ref = refs
    else:
        msg_ref, hi_ref, lo_ref, weights_ref, out_ref, grid_ref, state_ref, vt_ref, x_ref = refs
    vt_ref[...] = jnp.zeros(vt_ref.shape, F32)
    x_ref[...] = jnp.zeros(x_ref.shape, F32)
    for j in range(MSG_ROWS):
        vt_ref[j * 128 : (j + 1) * 128, 0:BLK] = jnp.transpose(
            msg_ref[pl.ds(j, BLK, stride=MSG_ROWS), :]
        )
    for sc in range(SC):
        for column in range(NLO):
            x_ref[column * CYC_PAD : column * CYC_PAD + CYC, sc * BLK : (sc + 1) * BLK] = vt_ref[
                pl.ds(sc * NLO + column, CYC, stride=LANES), 0:BLK
            ]
    dots = jnp.sum(vt_ref[CYC * LANES : (CYC + 2) * LANES, 0:BLK], axis=1, keepdims=True)

    def total(start, step):
        value = dots[start : start + NLO]
        for at in range(start + step, start + LANES, step):
            value = value + dots[at : at + NLO]
        return value

    fit = total(0, NLO)
    prior_zz = total(LANES, 2 * NLO)
    if later:
        prior_zd = total(LANES + NLO, 2 * NLO)
    trig = hi_ref[...], lo_ref[...]
    field = dot_split(x_ref[...], trig, NN)
    if later:
        beta = fit / state_ref[0:NLO, 0:1]
        prior_term = prior_zz + 2.0 * beta * prior_zd + beta * beta * state_ref[NLO : 2 * NLO, 0:1]
        spread_beta = jnp.concatenate(
            [jnp.broadcast_to(beta[i : i + 1], (CYC_PAD, 1)) for i in range(NLO)], axis=0
        )
        field = field + spread_beta * old_ref[...]
    else:
        beta = jnp.zeros_like(fit)
        prior_term = prior_zz
        grid_ref[...] = field
        state_ref[...] = jnp.broadcast_to(jnp.concatenate([fit, prior_term], axis=0), state_ref.shape)
    weights = weights_ref[...]
    weighted = jnp.concatenate(
        [field[i * CYC_PAD : (i + 1) * CYC_PAD] * weights for i in range(NLO)], axis=0
    )
    square = jnp.sum(weighted * field, axis=1, keepdims=True)
    energy = jnp.concatenate(
        [
            jnp.sum(square[i * CYC_PAD : (i + 1) * CYC_PAD], axis=0, keepdims=True)
            for i in range(NLO)
        ],
        axis=0,
    )
    spectrum = dot_split(weighted, trig, NT)
    extras_hi = jnp.broadcast_to(jnp.concatenate([energy] * SC, axis=0), (LANES, BLK))
    extras_lo = jnp.broadcast_to(
        jnp.concatenate([fit, prior_term, beta] + [jnp.zeros_like(fit)] * (SC - 3), axis=0),
        (LANES, BLK),
    )
    spread_rows(spectrum, vt_ref, extras_hi, extras_lo)
    write_messages(vt_ref, out_ref)


def unpack_kernel(msg_ref, out_ref, yt_ref):
    yt_ref[NR:, :] = jnp.zeros((128, 128), F32)
    for j in range(MSG_ROWS):
        value = msg_ref[pl.ds(j, BLK, stride=MSG_ROWS), :]
        for q in range(128 // LANES):
            cycle = 4 * j + q
            turned = value if q == 0 else pltpu.roll(value, 128 - q * LANES, 1)
            if cycle < CYC:
                yt_ref[pl.ds(cycle, BLK, stride=CYC), :] = turned
            elif cycle == CYC:
                yt_ref[NR : NR + 1, :] = jnp.sum(turned, axis=0, keepdims=True)
            else:
                yt_ref[NR + 1 : NR + 2, :] = turned[0:1]
    for t in range(TILES):
        turned = jnp.transpose(yt_ref[t * 128 : (t + 1) * 128, :])
        out_ref[t * LANES : (t + 1) * LANES, :] = turned[:LANES]
    tail = jnp.transpose(yt_ref[NR:, :])[:LANES]
    energy = tail[:SIZE, 0:1]
    fit, prior_term, beta = (
        jnp.concatenate([tail[i * NLO : (i + 1) * NLO, 1:2]] * 2, axis=0) for i in range(3)
    )
    alpha = fit / (energy + prior_term)
    lane = lax.broadcasted_iota(jnp.int32, (SIZE, 128), 1)
    out_ref[EXTRA:, :] = jnp.where(lane == 0, alpha, jnp.where(lane == 1, beta, 0.0))


def pack_kernel(y0, y1, y2, y3, out_ref, yt_ref):
    for t in range(TILES + 1):
        rows = slice(t * LANES, t * LANES + (LANES if t < TILES else SIZE))
        total = y0[rows, :] + y1[rows, :] + y2[rows, :] + y3[rows, :]
        if t == TILES:
            total = jnp.concatenate([total, jnp.zeros((LANES - SIZE, 128), F32)], axis=0)
        yt_ref[t * 128 : (t + 1) * 128, 0:LANES] = jnp.transpose(total)
    for j in range(MSG_ROWS):
        pieces = []
        for q in range(128 // LANES):
            cycle = 4 * j + q
            if cycle < CYC:
                pieces.append(yt_ref[pl.ds(cycle, BLK, stride=CYC), 0:LANES])
            else:
                at = NR + cycle - CYC
                pieces.append(jnp.broadcast_to(yt_ref[at : at + 1, 0:LANES], (BLK, LANES)))
        out_ref[pl.ds(j, BLK, stride=MSG_ROWS), :] = jnp.concatenate(pieces, axis=1)


def prepare_kernel(
    legendre_ref, precond_ref, hi, lo, turned_hi, turned_lo, p_hi, p_lo, done_ref, held, sems
):
    starts = list(range(0, DEG, PREP_STEP))

    def copies(i):
        count = min(PREP_STEP, DEG - starts[i])
        return [
            pltpu.make_async_copy(
                legendre_ref.at[pl.ds(starts[i], count), :, pl.ds(t * 128, 128)],
                held.at[i % 2, t, pl.ds(0, count)],
                sems.at[i % 2, t],
            )
            for t in range(TILES)
        ]

    for copy in copies(0):
        copy.start()
    for i, start in enumerate(starts):
        if i + 1 < len(starts):
            for copy in copies(i + 1):
                copy.start()
        for copy in copies(i):
            copy.wait()
        count = min(PREP_STEP, DEG - start)
        for t in range(TILES):
            flat = held.at[i % 2, t].reshape(PREP_STEP * SLOTS, 128)
            cols = slice(t * 128, (t + 1) * 128)
            for slot in range(SLOTS):
                value = flat[pl.ds(slot, count, stride=SLOTS), :]
                hi[slot, start : start + count, cols], lo[slot, start : start + count, cols] = split(value)
                turned = split(jnp.transpose(value))
                turned_hi[slot, cols, start : start + count] = turned[0]
                turned_lo[slot, cols, start : start + count] = turned[1]
    for slot in range(SLOTS):
        for g in range(GROUPS):
            p_hi[slot, g], p_lo[slot, g] = split(precond_ref[slot, g])
    done_ref[...] = jnp.zeros(done_ref.shape, F32)


def coefficient_kernel(stage, assign_ref, *refs):
    refs = list(refs)
    take = lambda: refs.pop(0)
    chunks = [take() for _ in range(LON)]
    hi_ref, lo_ref, turned_hi, turned_lo, prior_ref = (take() for _ in range(5))
    if stage != "last":
        p_hi, p_lo = take(), take()
    if stage == "middle":
        res_ref, d_ref = take(), take()
    if stage == "last":
        res_ref, z_ref, d_ref, old_alpha_ref, sol_out, res_out = (take() for _ in range(6))
    else:
        res_out, z_out = take(), take()
        y_refs = [take() for _ in range(LON)]
    if stage == "middle":
        alpha_out = take()

    lon = lax.axis_index("lon")
    first_slot = lax.axis_index("blk") * SLOTS
    degree = lon * DEG + lax.broadcasted_iota(jnp.int32, (ROWS, DEG), 1)
    row = lax.broadcasted_iota(jnp.int32, (ROWS, DEG), 0)
    sine = lax.rem(row // NLO, 2) == 1
    prior = prior_ref[...]
    extras = jnp.concatenate([chunk[EXTRA:, :] for chunk in chunks], axis=0)
    alpha, beta = extras[:, 0:1], extras[:, 1:2]
    fit = prior_zz = prior_zd = jnp.zeros((ROWS, 1), F32)

    for slot in range(SLOTS):
        order = assign_ref[first_slot + slot] * 8
        dead_sine = jnp.logical_and(sine, order == 0)
        live = jnp.logical_and(degree >= order, jnp.logical_not(dead_sine))
        cycles = jnp.concatenate(
            [
                jnp.concatenate(
                    [
                        chunk[t * LANES + slot * SIZE : t * LANES + (slot + 1) * SIZE, :]
                        for chunk in chunks
                    ],
                    axis=0,
                )
                for t in range(TILES)
            ],
            axis=1,
        )
        image = dot_split(cycles, (turned_hi[slot], turned_lo[slot]), NN)

        if stage == "last":
            old = d_ref[slot]
            direction = z_ref[slot] + beta * old
            image = jnp.where(live, image + prior * direction, 0.0)
            fitted = old_alpha_ref[:, 0:1] * old + alpha * direction
            residual = res_ref[slot] - alpha * image
            for out, value in ((sol_out, fitted), (res_out, residual)):
                parts = [value[i * SIZE : (i + 1) * SIZE] for i in range(LON)]
                for place in range(LON):
                    shift = lax.rem(place - lon + LON, LON)
                    chosen = parts[0]
                    for i in range(1, LON):
                        chosen = jnp.where(shift == i, parts[i], chosen)
                    for part in range(2):
                        out[slot, part, place * NLO : (place + 1) * NLO, :] = chosen[
                            part * NLO : (part + 1) * NLO
                        ]
            continue

        if stage == "first":
            residual = jnp.where(live, image, 0.0)
        else:
            old = d_ref[slot]
            image = jnp.where(live, image + prior * old, 0.0)
            residual = res_ref[slot] - alpha * image
        applied = [
            dot_split(
                residual[:, g * BLOCK : (g + 1) * BLOCK], (p_hi[slot, g], p_lo[slot, g]), NT
            )
            for g in range(GROUPS)
        ]
        search = jnp.where(live, jnp.concatenate(applied, axis=1), 0.0)
        res_out[slot] = residual
        z_out[slot] = search
        up = dot_split(search, (hi_ref[slot], lo_ref[slot]), NN)
        for shift, y_ref in enumerate(y_refs):
            for t in range(TILES):
                at = t * LANES + slot * SIZE
                y_ref[at : at + SIZE, :] = up[
                    shift * SIZE : (shift + 1) * SIZE, t * 128 : (t + 1) * 128
                ]
        fit = fit + jnp.sum(residual * search, axis=1, keepdims=True)
        prior_zz = prior_zz + jnp.sum(search * prior * search, axis=1, keepdims=True)
        if stage == "middle":
            prior_zd = prior_zd + jnp.sum(search * prior * old, axis=1, keepdims=True)

    if stage == "last":
        return
    if stage == "middle":
        alpha_out[...] = jnp.broadcast_to(alpha, (ROWS, 128))
    lane = lax.broadcasted_iota(jnp.int32, (SIZE, 128), 1)
    for shift, y_ref in enumerate(y_refs):
        at = shift * SIZE
        both = jnp.concatenate(
            [
                prior_zz[at : at + NLO] + prior_zz[at + NLO : at + SIZE],
                prior_zd[at : at + NLO] + prior_zd[at + NLO : at + SIZE],
            ],
            axis=0,
        )
        y_ref[EXTRA:, :] = jnp.where(
            lane == 0, fit[at : at + SIZE], jnp.where(lane == 1, both, 0.0)
        )


def coefficient_step(stage, assign, chunks, arrays):
    state = shape(SLOTS, ROWS, DEG)
    if stage == "last":
        out_shape = [shape(SLOTS, 2, NRHS, DEG)] * 2
    else:
        out_shape = [state] * 2 + [shape(CHUNK_ROWS, 128)] * LON
    if stage == "middle":
        out_shape.append(shape(ROWS, 128))
    operands = [*chunks, *arrays]
    return call(
        functools.partial(coefficient_kernel, stage),
        out_shape,
        in_specs=[pl.BlockSpec(memory_space=pltpu.SMEM)]
        + [pl.BlockSpec(memory_space=pltpu.VMEM)] * len(operands),
    )(assign, *operands)


def give_chunks(chunks):
    moved = [lax.ppermute(c, "lon", perm) for c, perm in zip(chunks[1:], PERMS)]
    return [chunks[0]] + moved


def gather_chunks(chunk):
    moved = [lax.ppermute(chunk, "lon", perm) for perm in PERMS]
    return [chunk] + moved[::-1]


def exchange(messages):
    sent = messages.reshape(BLK, 1, MSG_ROWS * 128)
    return lax.all_to_all(sent, "blk", 0, 0, tiled=True).reshape(BLK * MSG_ROWS, 128)


def trig_table(assign):
    index = assign.reshape(BLK, SLOTS).T.reshape(SLOTS, 1, BLK, 1) * 8
    column = jnp.arange(PERIOD_PAD, dtype=jnp.int32)
    angles = ((index * column) % (8 * PERIOD)).astype(F32) * (2.0 * math.pi / (8 * PERIOD))
    table = jnp.concatenate([jnp.cos(angles), jnp.sin(angles)], axis=1)
    table = jnp.where(column < PERIOD, table, 0.0).reshape(SC * BLK, PERIOD_PAD)
    coarse = lax.reduce_precision(table, 8, 7)
    return coarse.astype(BF16), (table - coarse).astype(BF16)


def body(anomalies, classes, legendre, precond, prior, assign):
    trig = trig_table(assign)
    prior_row = prior.reshape(1, DEG)
    messages = shape(BLK * MSG_ROWS, 128)
    vt = pltpu.VMEM((MSG_ROWS * 128, 128), F32)
    yt = pltpu.VMEM((NR + 128, 128), F32)
    grid_rows = NLO * CYC_PAD
    x_scratch = pltpu.VMEM((grid_rows, SC * BLK), F32)
    vmem = pl.BlockSpec(memory_space=pltpu.VMEM)

    folded = call(
        fold_kernel,
        [shape(grid_rows, PERIOD_PAD)] * LON,
        [pltpu.VMEM((NRHS, CYC_PAD, PERIOD_PAD), F32)],
    )(jnp.transpose(anomalies, (1, 0, 2)), classes)
    folded = give_chunks(folded)
    direct = jax.ShapeDtypeStruct((SLOTS, DEG, NR), BF16)
    turned = jax.ShapeDtypeStruct((SLOTS, NR, DEG), BF16)
    blocks = jax.ShapeDtypeStruct(precond.shape, BF16)
    *prepared, done = call(
        prepare_kernel,
        [direct, direct, turned, turned, blocks, blocks, shape(8, 128)],
        [
            pltpu.VMEM((2, TILES, PREP_STEP, SLOTS, 128), F32),
            pltpu.SemaphoreType.DMA((2, TILES)),
        ],
        in_specs=[pl.BlockSpec(memory_space=pl.ANY), vmem],
        out_specs=[vmem] * 7,
    )(jnp.transpose(legendre, (1, 0, 2)), precond)

    sent, weights = call(first_kernel, [messages, shape(CYC_PAD, PERIOD_PAD)], [vt])(
        *folded, *trig, done
    )

    def to_coefficients(received):
        return gather_chunks(call(unpack_kernel, shape(CHUNK_ROWS, 128), [yt])(received))

    def to_grid(chunks):
        return exchange(call(pack_kernel, messages, [yt])(*give_chunks(chunks)))

    basis = [*prepared[:4], prior_row]
    blocks = prepared[4:]
    res0, z0, *chunks = coefficient_step(
        "first", assign, to_coefficients(exchange(sent)), [*basis, *blocks]
    )
    sent, field, state = call(
        functools.partial(grid_kernel, False),
        [messages, shape(grid_rows, PERIOD_PAD), shape(2 * NLO, 128)],
        [vt, x_scratch],
    )(to_grid(chunks), *trig, weights)
    res1, z1, *chunks, alpha0 = coefficient_step(
        "middle", assign, to_coefficients(exchange(sent)), [*basis, *blocks, res0, z0]
    )
    sent = call(functools.partial(grid_kernel, True), messages, [vt, x_scratch])(
        to_grid(chunks), *trig, weights, field, state
    )
    return tuple(
        coefficient_step(
            "last", assign, to_coefficients(exchange(sent)), [*basis, res1, z1, z0, alpha0]
        )
    )


def solution(mesh):
    in_specs = (
        P(None, "blk", "lon"),
        P("blk", "lon"),
        P("blk", "lon", None),
        P("blk", "lon", None, None),
        P("lon"),
        P(),
    )
    out_specs = (P("blk", None, None, "lon"), P("blk", None, None, "lon"))
    return jax.shard_map(body, mesh=mesh, in_specs=in_specs, out_specs=out_specs, check_vma=False)
```

```python
import functools
import math

import jax
import jax.numpy as jnp
from jax import lax
from jax.experimental import pallas as pl
from jax.experimental.pallas import tpu as pltpu
from jax.sharding import PartitionSpec as P

F32 = jnp.float32
BF16 = jnp.bfloat16
HUBER_LEVELS = (1.0, 0.5, 0.25, 0.125)

BLK = 64
LON = 4
SLOTS = 4
NRHS = 16
NLO = NRHS // LON
CYC = 18
CYC_PAD = 24
PERIOD = 540
PERIOD_PAD = 640
DEG = 540
NR = BLK * CYC
BLOCK = 135
GROUPS = DEG // BLOCK
SC = 2 * SLOTS
LANES = SC * NLO
MSG_ROWS = 5
TILES = NR // 128
SIZE = 2 * NLO
ROWS = LON * SIZE
EXTRA = TILES * LANES
CHUNK_ROWS = EXTRA + SIZE
PREP_STEP = 128
VMEM_LIMIT = 12 * 1024 * 1024
WALK_LIMITS = 40 * 1024 * 1024, 28 * 1024 * 1024
NN = (((1,), (0,)), ((), ()))
NT = (((1,), (1,)), ((), ()))
PERMS = [[(i, (i + s) % LON) for i in range(LON)] for s in range(1, LON)]


def split(x):
    hi = x.astype(BF16)
    return hi, (x - hi.astype(F32)).astype(BF16)


def dot(a, b, dims):
    return lax.dot_general(a, b, dims, preferred_element_type=F32)


def dot_split(a, b, dims):
    b_hi, b_lo = b
    a_hi, a_lo = split(a)
    rows = a.shape[0]
    both = dot(jnp.concatenate([a_hi, a_lo], axis=0), b_hi, dims)
    return both[:rows] + both[rows:] + dot(a_hi, b_lo, dims)


def call(kernel, out_shape, scratch=(), limit=VMEM_LIMIT, **kw):
    return pl.pallas_call(
        kernel,
        out_shape=out_shape,
        scratch_shapes=list(scratch),
        compiler_params=pltpu.CompilerParams(vmem_limit_bytes=limit),
        **kw,
    )


def shape(*dims):
    return jax.ShapeDtypeStruct(dims, F32)


def fold_kernel(anomalies_ref, classes_ref, *refs):
    out_refs, by_column = refs[:-1], refs[-1]
    lon = lax.axis_index("lon")
    classes = classes_ref[...]
    weights = jnp.zeros(classes.shape, F32)
    for level, value in enumerate(HUBER_LEVELS):
        weights = weights + jnp.where(classes == level, value, 0.0)

    def fold(field):
        return field[:, :PERIOD] + field[:, PERIOD:]

    by_column[...] = jnp.zeros(by_column.shape, F32)
    for cycle in range(CYC):
        columns = fold(anomalies_ref[cycle] * weights[cycle : cycle + 1])
        for column in range(NRHS):
            by_column[column, cycle : cycle + 1, :PERIOD] = columns[column : column + 1]
    folded_weights = fold(weights)
    for shift, out in enumerate(out_refs):
        group = lax.rem(lon + shift, LON)
        for column in range(NLO):
            row = column * CYC_PAD
            out[row : row + CYC_PAD, :] = by_column[group * NLO + column]
            if column < CYC // 6:
                out[row + CYC : row + CYC_PAD, :PERIOD] = folded_weights[column * 6 : column * 6 + 6]


def spread_rows(values, vt_ref, extras_hi, extras_lo):
    for sc in range(SC):
        for column in range(NLO):
            piece = values[column * CYC_PAD : column * CYC_PAD + CYC, sc * BLK : (sc + 1) * BLK]
            vt_ref[pl.ds(sc * NLO + column, CYC, stride=LANES), 0:BLK] = piece
    vt_ref[CYC * LANES : (CYC + 1) * LANES, 0:BLK] = extras_hi
    vt_ref[(CYC + 1) * LANES : (CYC + 2) * LANES, 0:BLK] = extras_lo


def write_messages(vt_ref, out_ref):
    for j in range(MSG_ROWS):
        turned = jnp.transpose(vt_ref[j * 128 : (j + 1) * 128, :])
        out_ref[pl.ds(j, BLK, stride=MSG_ROWS), :] = turned[:BLK]


def first_kernel(c0, c1, c2, c3, hi_ref, lo_ref, done_ref, out_ref, weights_ref, vt_ref):
    total = c0[...] + c1[...] + c2[...] + c3[...]
    weights_ref[...] = jnp.zeros(weights_ref.shape, F32)
    for part in range(CYC // 6):
        weights_ref[part * 6 : part * 6 + 6, :] = total[
            part * CYC_PAD + CYC : (part + 1) * CYC_PAD
        ]
    spectrum = dot_split(total, (hi_ref[...], lo_ref[...]), NT)
    zero = jnp.zeros((LANES, BLK), F32)
    vt_ref[...] = jnp.zeros(vt_ref.shape, F32)
    spread_rows(spectrum, vt_ref, zero, zero)
    write_messages(vt_ref, out_ref)


def grid_kernel(later, *refs):
    if later:
        msg_ref, hi_ref, lo_ref, weights_ref, old_ref, state_ref, out_ref, vt_ref, x_ref = refs
    else:
        msg_ref, hi_ref, lo_ref, weights_ref, out_ref, grid_ref, state_ref, vt_ref, x_ref = refs
    vt_ref[...] = jnp.zeros(vt_ref.shape, F32)
    x_ref[...] = jnp.zeros(x_ref.shape, F32)
    for j in range(MSG_ROWS):
        vt_ref[j * 128 : (j + 1) * 128, 0:BLK] = jnp.transpose(
            msg_ref[pl.ds(j, BLK, stride=MSG_ROWS), :]
        )
    for sc in range(SC):
        for column in range(NLO):
            x_ref[column * CYC_PAD : column * CYC_PAD + CYC, sc * BLK : (sc + 1) * BLK] = vt_ref[
                pl.ds(sc * NLO + column, CYC, stride=LANES), 0:BLK
            ]
    dots = jnp.sum(vt_ref[CYC * LANES : (CYC + 2) * LANES, 0:BLK], axis=1, keepdims=True)

    def total(start, step):
        value = dots[start : start + NLO]
        for at in range(start + step, start + LANES, step):
            value = value + dots[at : at + NLO]
        return value

    fit = total(0, NLO)
    prior_zz = total(LANES, 2 * NLO)
    if later:
        prior_zd = total(LANES + NLO, 2 * NLO)
    trig = hi_ref[...], lo_ref[...]
    field = dot_split(x_ref[...], trig, NN)
    if later:
        beta = fit / state_ref[0:NLO, 0:1]
        prior_term = prior_zz + 2.0 * beta * prior_zd + beta * beta * state_ref[NLO : 2 * NLO, 0:1]
        spread_beta = jnp.concatenate(
            [jnp.broadcast_to(beta[i : i + 1], (CYC_PAD, 1)) for i in range(NLO)], axis=0
        )
        field = field + spread_beta * old_ref[...]
    else:
        beta = jnp.zeros_like(fit)
        prior_term = prior_zz
        grid_ref[...] = field
        state_ref[...] = jnp.broadcast_to(jnp.concatenate([fit, prior_term], axis=0), state_ref.shape)
    weights = weights_ref[...]
    weighted = jnp.concatenate(
        [field[i * CYC_PAD : (i + 1) * CYC_PAD] * weights for i in range(NLO)], axis=0
    )
    square = jnp.sum(weighted * field, axis=1, keepdims=True)
    energy = jnp.concatenate(
        [
            jnp.sum(square[i * CYC_PAD : (i + 1) * CYC_PAD], axis=0, keepdims=True)
            for i in range(NLO)
        ],
        axis=0,
    )
    spectrum = dot_split(weighted, trig, NT)
    extras_hi = jnp.broadcast_to(jnp.concatenate([energy] * SC, axis=0), (LANES, BLK))
    extras_lo = jnp.broadcast_to(
        jnp.concatenate([fit, prior_term, beta] + [jnp.zeros_like(fit)] * (SC - 3), axis=0),
        (LANES, BLK),
    )
    spread_rows(spectrum, vt_ref, extras_hi, extras_lo)
    write_messages(vt_ref, out_ref)


def unpack_kernel(msg_ref, out_ref, yt_ref):
    yt_ref[NR:, :] = jnp.zeros((128, 128), F32)
    for j in range(MSG_ROWS):
        value = msg_ref[pl.ds(j, BLK, stride=MSG_ROWS), :]
        for q in range(128 // LANES):
            cycle = 4 * j + q
            turned = value if q == 0 else pltpu.roll(value, 128 - q * LANES, 1)
            if cycle < CYC:
                yt_ref[pl.ds(cycle, BLK, stride=CYC), :] = turned
            elif cycle == CYC:
                yt_ref[NR : NR + 1, :] = jnp.sum(turned, axis=0, keepdims=True)
            else:
                yt_ref[NR + 1 : NR + 2, :] = turned[0:1]
    for t in range(TILES):
        turned = jnp.transpose(yt_ref[t * 128 : (t + 1) * 128, :])
        out_ref[t * LANES : (t + 1) * LANES, :] = turned[:LANES]
    tail = jnp.transpose(yt_ref[NR:, :])[:LANES]
    energy = tail[:SIZE, 0:1]
    fit, prior_term, beta = (
        jnp.concatenate([tail[i * NLO : (i + 1) * NLO, 1:2]] * 2, axis=0) for i in range(3)
    )
    alpha = fit / (energy + prior_term)
    lane = lax.broadcasted_iota(jnp.int32, (SIZE, 128), 1)
    out_ref[EXTRA:, :] = jnp.where(lane == 0, alpha, jnp.where(lane == 1, beta, 0.0))


def pack_kernel(y0, y1, y2, y3, *refs):
    out_ref, yt_ref = refs[-2:]
    for t in range(TILES + 1):
        rows = slice(t * LANES, t * LANES + (LANES if t < TILES else SIZE))
        total = y0[rows, :] + y1[rows, :] + y2[rows, :] + y3[rows, :]
        if t == TILES:
            total = jnp.concatenate([total, jnp.zeros((LANES - SIZE, 128), F32)], axis=0)
        yt_ref[t * 128 : (t + 1) * 128, 0:LANES] = jnp.transpose(total)
    for j in range(MSG_ROWS):
        pieces = []
        for q in range(128 // LANES):
            cycle = 4 * j + q
            if cycle < CYC:
                pieces.append(yt_ref[pl.ds(cycle, BLK, stride=CYC), 0:LANES])
            else:
                at = NR + cycle - CYC
                pieces.append(jnp.broadcast_to(yt_ref[at : at + 1, 0:LANES], (BLK, LANES)))
        out_ref[pl.ds(j, BLK, stride=MSG_ROWS), :] = jnp.concatenate(pieces, axis=1)


def walk_legendre(legendre_ref, held, sems, use):
    starts = list(range(0, DEG, PREP_STEP))

    def copies(i):
        count = min(PREP_STEP, DEG - starts[i])
        return [
            pltpu.make_async_copy(
                legendre_ref.at[pl.ds(starts[i], count), :, pl.ds(t * 128, 128)],
                held.at[i % 2, t, pl.ds(0, count)],
                sems.at[i % 2, t],
            )
            for t in range(TILES)
        ]

    for copy in copies(0):
        copy.start()
    for i, start in enumerate(starts):
        if i + 1 < len(starts):
            for copy in copies(i + 1):
                copy.start()
        for copy in copies(i):
            copy.wait()
        count = min(PREP_STEP, DEG - start)
        for t in range(TILES):
            flat = held.at[i % 2, t].reshape(PREP_STEP * SLOTS, 128)
            for slot in range(SLOTS):
                value = flat[pl.ds(slot, count, stride=SLOTS), :]
                use(slot, slice(start, start + count), slice(t * 128, (t + 1) * 128), value)


def direct_kernel(legendre_ref, hi, lo, done_ref, held, sems):
    def use(slot, degrees, cycles, value):
        hi[slot, degrees, cycles], lo[slot, degrees, cycles] = split(value)

    walk_legendre(legendre_ref, held, sems, use)
    done_ref[...] = jnp.zeros(done_ref.shape, F32)


def turned_kernel(legendre_ref, after_ref, hi, lo, done_ref, held, sems):
    def use(slot, degrees, cycles, value):
        hi[slot, cycles, degrees], lo[slot, cycles, degrees] = split(jnp.transpose(value))

    walk_legendre(legendre_ref, held, sems, use)
    done_ref[...] = jnp.zeros(done_ref.shape, F32)


def blocks_kernel(precond_ref, after_ref, p_hi, p_lo):
    for slot in range(SLOTS):
        for g in range(GROUPS):
            p_hi[slot, g], p_lo[slot, g] = split(precond_ref[slot, g])


def coefficient_kernel(stage, assign_ref, *refs):
    refs = list(refs)
    take = lambda: refs.pop(0)
    chunks = [take() for _ in range(LON)]
    hi_ref, lo_ref, prior_ref = take(), take(), take()
    if stage != "first":
        turned_hi, turned_lo = take(), take()
    if stage != "last":
        p_hi, p_lo = take(), take()
    if stage == "middle":
        res_ref, d_ref = take(), take()
    if stage == "last":
        res_ref, z_ref, d_ref, old_alpha_ref, sol_out, res_out = (take() for _ in range(6))
    else:
        res_out, z_out = take(), take()
        y_refs = [take() for _ in range(LON)]
    if stage == "middle":
        alpha_out = take()

    lon = lax.axis_index("lon")
    first_slot = lax.axis_index("blk") * SLOTS
    degree = lon * DEG + lax.broadcasted_iota(jnp.int32, (ROWS, DEG), 1)
    row = lax.broadcasted_iota(jnp.int32, (ROWS, DEG), 0)
    sine = lax.rem(row // NLO, 2) == 1
    prior = prior_ref[...]
    extras = jnp.concatenate([chunk[EXTRA:, :] for chunk in chunks], axis=0)
    alpha, beta = extras[:, 0:1], extras[:, 1:2]
    fit = prior_zz = prior_zd = jnp.zeros((ROWS, 1), F32)

    for slot in range(SLOTS):
        order = assign_ref[first_slot + slot] * 8
        dead_sine = jnp.logical_and(sine, order == 0)
        live = jnp.logical_and(degree >= order, jnp.logical_not(dead_sine))
        cycles = jnp.concatenate(
            [
                jnp.concatenate(
                    [
                        chunk[t * LANES + slot * SIZE : t * LANES + (slot + 1) * SIZE, :]
                        for chunk in chunks
                    ],
                    axis=0,
                )
                for t in range(TILES)
            ],
            axis=1,
        )
        if stage == "first":
            x_hi, x_lo = split(cycles)
            both = dot(hi_ref[slot], jnp.concatenate([x_hi, x_lo], axis=0), NT)
            image = jnp.transpose(both[:, :ROWS] + both[:, ROWS:] + dot(lo_ref[slot], x_hi, NT))
        else:
            image = dot_split(cycles, (turned_hi[slot], turned_lo[slot]), NN)

        if stage == "last":
            old = d_ref[slot]
            direction = z_ref[slot] + beta * old
            image = jnp.where(live, image + prior * direction, 0.0)
            fitted = old_alpha_ref[:, 0:1] * old + alpha * direction
            residual = res_ref[slot] - alpha * image
            for out, value in ((sol_out, fitted), (res_out, residual)):
                parts = [value[i * SIZE : (i + 1) * SIZE] for i in range(LON)]
                for place in range(LON):
                    shift = lax.rem(place - lon + LON, LON)
                    chosen = parts[0]
                    for i in range(1, LON):
                        chosen = jnp.where(shift == i, parts[i], chosen)
                    for part in range(2):
                        out[slot, part, place * NLO : (place + 1) * NLO, :] = chosen[
                            part * NLO : (part + 1) * NLO
                        ]
            continue

        if stage == "first":
            residual = jnp.where(live, image, 0.0)
        else:
            old = d_ref[slot]
            image = jnp.where(live, image + prior * old, 0.0)
            residual = res_ref[slot] - alpha * image
        applied = [
            dot_split(
                residual[:, g * BLOCK : (g + 1) * BLOCK], (p_hi[slot, g], p_lo[slot, g]), NT
            )
            for g in range(GROUPS)
        ]
        search = jnp.where(live, jnp.concatenate(applied, axis=1), 0.0)
        res_out[slot] = residual
        z_out[slot] = search
        up = dot_split(search, (hi_ref[slot], lo_ref[slot]), NN)
        for shift, y_ref in enumerate(y_refs):
            for t in range(TILES):
                at = t * LANES + slot * SIZE
                y_ref[at : at + SIZE, :] = up[
                    shift * SIZE : (shift + 1) * SIZE, t * 128 : (t + 1) * 128
                ]
        fit = fit + jnp.sum(residual * search, axis=1, keepdims=True)
        prior_zz = prior_zz + jnp.sum(search * prior * search, axis=1, keepdims=True)
        if stage == "middle":
            prior_zd = prior_zd + jnp.sum(search * prior * old, axis=1, keepdims=True)

    if stage == "last":
        return
    if stage == "middle":
        alpha_out[...] = jnp.broadcast_to(alpha, (ROWS, 128))
    lane = lax.broadcasted_iota(jnp.int32, (SIZE, 128), 1)
    for shift, y_ref in enumerate(y_refs):
        at = shift * SIZE
        both = jnp.concatenate(
            [
                prior_zz[at : at + NLO] + prior_zz[at + NLO : at + SIZE],
                prior_zd[at : at + NLO] + prior_zd[at + NLO : at + SIZE],
            ],
            axis=0,
        )
        y_ref[EXTRA:, :] = jnp.where(
            lane == 0, fit[at : at + SIZE], jnp.where(lane == 1, both, 0.0)
        )


def coefficient_step(stage, assign, chunks, arrays):
    state = shape(SLOTS, ROWS, DEG)
    if stage == "last":
        out_shape = [shape(SLOTS, 2, NRHS, DEG)] * 2
    else:
        out_shape = [state] * 2 + [shape(CHUNK_ROWS, 128)] * LON
    if stage == "middle":
        out_shape.append(shape(ROWS, 128))
    operands = [*chunks, *arrays]
    return call(
        functools.partial(coefficient_kernel, stage),
        out_shape,
        in_specs=[pl.BlockSpec(memory_space=pltpu.SMEM)]
        + [pl.BlockSpec(memory_space=pltpu.VMEM)] * len(operands),
    )(assign, *operands)


def give_chunks(chunks):
    moved = [lax.ppermute(c, "lon", perm) for c, perm in zip(chunks[1:], PERMS)]
    return [chunks[0]] + moved


def gather_chunks(chunk):
    moved = [lax.ppermute(chunk, "lon", perm) for perm in PERMS]
    return [chunk] + moved[::-1]


def exchange(messages):
    sent = messages.reshape(BLK, 1, MSG_ROWS * 128)
    return lax.all_to_all(sent, "blk", 0, 0, tiled=True).reshape(BLK * MSG_ROWS, 128)


def trig_table(assign):
    index = assign.reshape(BLK, SLOTS).T.reshape(SLOTS, 1, BLK, 1) * 8
    column = jnp.arange(PERIOD_PAD, dtype=jnp.int32)
    angles = ((index * column) % (8 * PERIOD)).astype(F32) * (2.0 * math.pi / (8 * PERIOD))
    table = jnp.concatenate([jnp.cos(angles), jnp.sin(angles)], axis=1)
    table = jnp.where(column < PERIOD, table, 0.0).reshape(SC * BLK, PERIOD_PAD)
    coarse = lax.reduce_precision(table, 8, 7)
    return coarse.astype(BF16), (table - coarse).astype(BF16)


def body(anomalies, classes, legendre, precond, prior, assign):
    trig = trig_table(assign)
    prior_row = prior.reshape(1, DEG)
    messages = shape(BLK * MSG_ROWS, 128)
    vt = pltpu.VMEM((MSG_ROWS * 128, 128), F32)
    yt = pltpu.VMEM((NR + 128, 128), F32)
    grid_rows = NLO * CYC_PAD
    x_scratch = pltpu.VMEM((grid_rows, SC * BLK), F32)
    vmem = pl.BlockSpec(memory_space=pltpu.VMEM)

    folded = call(
        fold_kernel,
        [shape(grid_rows, PERIOD_PAD)] * LON,
        [pltpu.VMEM((NRHS, CYC_PAD, PERIOD_PAD), F32)],
    )(jnp.transpose(anomalies, (1, 0, 2)), classes)
    folded = give_chunks(folded)
    direct = jax.ShapeDtypeStruct((SLOTS, DEG, NR), BF16)
    turned = jax.ShapeDtypeStruct((SLOTS, NR, DEG), BF16)
    blocks = jax.ShapeDtypeStruct(precond.shape, BF16)
    walk = [
        pltpu.VMEM((2, TILES, PREP_STEP, SLOTS, 128), F32),
        pltpu.SemaphoreType.DMA((2, TILES)),
    ]
    anywhere = pl.BlockSpec(memory_space=pl.ANY)
    by_degree = jnp.transpose(legendre, (1, 0, 2))
    *direct, done = call(
        direct_kernel,
        [direct, direct, shape(8, 128)],
        walk,
        limit=WALK_LIMITS[0],
        in_specs=[anywhere],
        out_specs=[vmem] * 3,
    )(by_degree)
    sent, weights = call(first_kernel, [messages, shape(CYC_PAD, PERIOD_PAD)], [vt])(
        *folded, *trig, done
    )

    def unpack(received):
        return call(unpack_kernel, shape(CHUNK_ROWS, 128), [yt])(received)

    def to_coefficients(received):
        return gather_chunks(unpack(received))

    def to_grid(chunks, *after):
        return exchange(call(pack_kernel, messages, [yt])(*give_chunks(chunks), *after))

    unpacked = unpack(exchange(sent))
    blocks = call(
        blocks_kernel, [blocks, blocks], in_specs=[vmem, anywhere], out_specs=[vmem] * 2
    )(precond, unpacked)
    basis = [*direct, prior_row]
    res0, z0, *chunks = coefficient_step(
        "first", assign, gather_chunks(unpacked), [*basis, *blocks]
    )
    *turned, done = call(
        turned_kernel,
        [turned, turned, shape(8, 128)],
        walk,
        limit=WALK_LIMITS[1],
        in_specs=[anywhere] * 2,
        out_specs=[vmem] * 3,
    )(by_degree, chunks[0])
    basis += turned
    sent, field, state = call(
        functools.partial(grid_kernel, False),
        [messages, shape(grid_rows, PERIOD_PAD), shape(2 * NLO, 128)],
        [vt, x_scratch],
    )(to_grid(chunks, done), *trig, weights)
    res1, z1, *chunks, alpha0 = coefficient_step(
        "middle", assign, to_coefficients(exchange(sent)), [*basis, *blocks, res0, z0]
    )
    sent = call(functools.partial(grid_kernel, True), messages, [vt, x_scratch])(
        to_grid(chunks), *trig, weights, field, state
    )
    return tuple(
        coefficient_step(
            "last", assign, to_coefficients(exchange(sent)), [*basis, res1, z1, z0, alpha0]
        )
    )


def solution(mesh):
    in_specs = (
        P(None, "blk", "lon"),
        P("blk", "lon"),
        P("blk", "lon", None),
        P("blk", "lon", None, None),
        P("lon"),
        P(),
    )
    out_specs = (P("blk", None, None, "lon"), P("blk", None, None, "lon"))
    return jax.shard_map(body, mesh=mesh, in_specs=in_specs, out_specs=out_specs, check_vma=False)
```
